32 devices in a mesh: row: 16 (over z, y, core), col: 2 (over x).
Axes of the slice: x: 2, y: 2, z: 4, core: 2. Of those that a mesh axis runs over, the one named last changes fastest.
Arguments:
- tokens: bfloat16 [512, 16384], P('row', 'col'), may hold values from -6 to 6
- cotangent: bfloat16 [512, 16384], P('row', 'col'), may hold values from -6 to 6
- w_gate: bfloat16 [16384, 12288], P('col', 'row'), may hold values from -0.046875 to 0.046875
- w_up: bfloat16 [16384, 12288], P('col', 'row'), may hold values from -0.046875 to 0.046875
- w_down: bfloat16 [12288, 16384], P('row', 'col'), may hold values from -0.0546875 to 0.0546875
Outputs:
- grad_tokens: bfloat16 [512, 16384], P('row', 'col')
- grad_w_gate: bfloat16 [16384, 12288], P('col', 'row')
- grad_w_up: bfloat16 [16384, 12288], P('col', 'row')
- grad_w_down: bfloat16 [12288, 16384], P('row', 'col')
The draws below stay inside these ranges and needn't reach their ends.
All inputs are finite; a program needn't handle non-finite values.
Results may differ from the reference program's by a relative error of at most 0.005.
Values may be sent and summed in bfloat16 or wider, within the bound.
No kernel may reach another device: no remote copies, remote signals or barrier semaphores. Data moves between devices by JAX's collectives and lax.ppermute only.
A program may use at most 192 MiB of HBM per device.

```python
import jax
import jax.numpy as jnp

D = 16384
FF = 12288
TOKENS = 512


def level_of(own_key, shape, cuts, low, high):
    def one(position, blocks):
        draws = jax.random.uniform(jax.random.fold_in(jax.random.fold_in(own_key, 6), position), (blocks,), jnp.float32, low / len(cuts), high / len(cuts))
        return jnp.repeat(jnp.exp(draws), shape[position] // blocks).reshape((-1,) + (1,) * (len(shape) - position - 1))

    loudness = one(*cuts[0])
    for cut in cuts[1:]:
        loudness = loudness * one(*cut)
    return loudness


def noise(stream_key, shape, spread, reach, pieces=(), held_as=jnp.bfloat16):
    entries = spread * jax.random.normal(stream_key, shape, jnp.float32)
    if pieces:
        entries = entries * level_of(stream_key, shape, pieces, -0.22, 0.18)
    return jnp.clip(entries, -reach, reach).astype(held_as)


def setup_inputs(seed: int = 0) -> dict:
    arg_keys = jax.random.split(jax.random.key(seed), 6)
    tokens = noise(arg_keys[0], (TOKENS, D), 1.0, 6.0, ((0, 16), (1, 2)))
    cotangent = noise(arg_keys[1], (TOKENS, D), 1.0, 6.0, ((0, 16), (1, 2)))
    w_gate = noise(arg_keys[2], (D, FF), D ** -0.5, 0.046875, ((0, 2), (1, 16)))
    w_up = noise(arg_keys[3], (D, FF), D ** -0.5, 0.046875, ((0, 2), (1, 16)))
    w_down = noise(arg_keys[4], (FF, D), FF ** -0.5, 0.0546875, ((0, 16), (1, 2)))
    return dict(tokens=tokens, cotangent=cotangent, w_gate=w_gate, w_up=w_up, w_down=w_down)


def reference(tokens, cotangent, w_gate, w_up, w_down):
    gate_value = jnp.dot(tokens, w_gate, preferred_element_type=jnp.float32)
    up_value = jnp.dot(tokens, w_up, preferred_element_type=jnp.float32)
    grad_act = jnp.dot(cotangent, w_down.T, preferred_element_type=jnp.float32)
    sigmoid_gate = jax.nn.sigmoid(gate_value)
    silu_gate = gate_value * sigmoid_gate
    activation = (silu_gate * up_value).astype(jnp.bfloat16)
    grad_gate = (grad_act * up_value * sigmoid_gate * (1.0 + gate_value * (1.0 - sigmoid_gate))).astype(jnp.bfloat16)
    grad_up = (grad_act * silu_gate).astype(jnp.bfloat16)
    grad_w_gate = jnp.dot(tokens.T, grad_gate, preferred_element_type=jnp.float32).astype(jnp.bfloat16)
    grad_w_up = jnp.dot(tokens.T, grad_up, preferred_element_type=jnp.float32).astype(jnp.bfloat16)
    grad_w_down = jnp.dot(activation.T, cotangent, preferred_element_type=jnp.float32).astype(jnp.bfloat16)
    grad_tokens = (jnp.dot(grad_gate, w_gate.T, preferred_element_type=jnp.float32) + jnp.dot(grad_up, w_up.T, preferred_element_type=jnp.float32)).astype(jnp.bfloat16)
    return grad_tokens, grad_w_gate, grad_w_up, grad_w_down
```

```python
import jax
import jax.numpy as jnp
from jax import lax
from jax.experimental import pallas as pl
from jax.experimental.pallas import tpu as pltpu
from jax.sharding import PartitionSpec as P

F32, BF16 = jnp.float32, jnp.bfloat16
MIB = 2**20
NT = (((1,), (1,)), ((), ()))
TN = (((0,), (0,)), ((), ()))
HBM = pl.BlockSpec(memory_space=pl.ANY)
VMEM = pl.BlockSpec(memory_space=pltpu.VMEM)


def dot(left, right):
    return jnp.dot(left, right, preferred_element_type=F32)


def dot_nt(left, right):
    return lax.dot_general(left, right, NT, preferred_element_type=F32)


def dot_tn(left, right):
    return lax.dot_general(left, right, TN, preferred_element_type=F32)


def tile_of(size, most):
    return most if size % most == 0 else size


def after(values, *earlier):
    return lax.optimization_barrier((values, earlier))[0]


def in_vmem(a):
    return pltpu.with_memory_space_constraint(a, pltpu.VMEM)


def in_hbm(a):
    return pltpu.with_memory_space_constraint(a, pltpu.HBM)


def cost(flops, nbytes):
    return pl.CostEstimate(flops=flops, bytes_accessed=nbytes, transcendentals=0)


def load_weights(w_gate, w_up, w_down):
    features, hidden = w_gate.shape
    tile = tile_of(features, 1024)
    steps = features // tile

    def body(gate, up, down, gate_out, up_out, down_out, piece, sem, piece_sem):
        whole = [
            pltpu.make_async_copy(gate, gate_out, sem.at[0]),
            pltpu.make_async_copy(up, up_out, sem.at[1]),
        ]
        pieces = [
            pltpu.make_async_copy(
                down.at[:, pl.ds(i * tile, tile)], piece.at[i % 2], piece_sem.at[i]
            )
            for i in range(steps)
        ]
        pieces[0].start()
        for copy in whole:
            copy.start()
        for i in range(steps):
            if i + 1 < steps:
                pieces[i + 1].start()
            pieces[i].wait()
            down_out[pl.ds(i * tile, tile), :] = piece[i % 2].T
        for copy in whole:
            copy.wait()

    return pl.pallas_call(
        body,
        in_specs=[HBM] * 3,
        out_specs=[VMEM] * 3,
        out_shape=[pltpu.VMEM((features, hidden), BF16)] * 3,
        scratch_shapes=[
            pltpu.VMEM((2, hidden, tile), BF16),
            pltpu.SemaphoreType.DMA((2,)),
            pltpu.SemaphoreType.DMA((steps,)),
        ],
        cost_estimate=cost(0, 6 * features * hidden),
        compiler_params=pltpu.CompilerParams(vmem_limit_bytes=8 * MIB),
        name="load_weights",
    )(in_hbm(w_gate), in_hbm(w_up), in_hbm(w_down))


def forward(xs, dys, per, w_gate, w_up, w_down_t):
    features, hidden = w_gate.shape
    rows = per * len(xs)
    tile = tile_of(features, 2048)
    steps = features // tile
    arrays = []
    for a, _ in xs + dys:
        if not any(a is b for b in arrays):
            arrays.append(a)
    place = [([a is b for b in arrays].index(True), r) for a, r in xs + dys]
    count = len(arrays)

    def body(*refs):
        sources = refs[:count]
        gate, up, down_t, own, rounded, held, sem = refs[count:]
        copies = []
        for k in range(steps):
            cut = pl.ds(k * tile, tile)
            for i, (a, r) in enumerate(place):
                copy = pltpu.make_async_copy(
                    sources[a].at[pl.ds(r * per, per), cut],
                    held.at[pl.ds(i * per, per), cut],
                    sem.at[k, i],
                )
                copy.start()
                copies.append(copy)
        for k in range(steps):
            cut = pl.ds(k * tile, tile)
            for i in range(len(place)):
                copies[k * len(place) + i].wait()
            for j, weight in enumerate((gate, up, down_t)):
                out = pl.ds(j * hidden, hidden)
                source = pl.ds(rows if j == 2 else 0, rows)
                part = dot(held[source, cut], weight[cut, :])
                if k == 0:
                    own[:, out] = part
                else:
                    own[:, out] += part
        rounded[...] = own[...].astype(BF16)

    return pl.pallas_call(
        body,
        in_specs=[HBM] * count + [VMEM] * 3,
        out_specs=[VMEM] * 2,
        out_shape=[
            jax.ShapeDtypeStruct((rows, 3 * hidden), F32),
            jax.ShapeDtypeStruct((rows, 3 * hidden), BF16),
        ],
        scratch_shapes=[
            pltpu.VMEM((2 * rows, features), BF16),
            pltpu.SemaphoreType.DMA((steps, len(place))),
        ],
        cost_estimate=cost(6 * rows * hidden * features, 6 * hidden * features),
        compiler_params=pltpu.CompilerParams(vmem_limit_bytes=12 * MIB),
        name="forward",
    )(*arrays, in_vmem(w_gate), in_vmem(w_up), in_vmem(w_down_t))


def backward(pairs, w_gate, w_up):
    features, hidden = w_gate.shape
    sizes = [own.shape[0] for own, _ in pairs]
    rows = sum(sizes)
    half, tile = rows // 2, tile_of(features, 1024)
    steps = features // tile
    starts = [sum(sizes[:i]) for i in range(len(sizes))]

    def body(*refs):
        sums, refs = refs[: 2 * len(pairs)], refs[2 * len(pairs) :]
        gate_w, up_w, gate_out, up_out, act_out, mine, theirs, held, held16, sem = refs
        for i, size in enumerate(sizes):
            own, other, at = sums[2 * i], sums[2 * i + 1], pl.ds(starts[i], size)

            def total(j, own=own, other=other):
                cut = pl.ds(j * hidden, hidden)
                return own[:, cut] + other[:, cut].astype(F32)

            gate_value, up_value, grad_act = total(0), total(1), total(2)
            sigmoid_gate = jax.nn.sigmoid(gate_value)
            silu_gate = gate_value * sigmoid_gate
            act_out[at, :] = (silu_gate * up_value).astype(BF16)
            up_out[at, :] = (grad_act * silu_gate).astype(BF16)
            gate_out[at, :] = (
                grad_act * up_value * sigmoid_gate * (1.0 + gate_value * (1.0 - sigmoid_gate))
            ).astype(BF16)
        copies = []
        for k in range(steps):
            cut = pl.ds(k * tile, tile)
            out = dot_nt(gate_out[...], gate_w[cut, :]) + dot_nt(up_out[...], up_w[cut, :])
            for start, size in zip(starts, sizes):
                to, middle = pl.ds(start // 2, size // 2), start + size // 2
                held[to, cut] = out[start:middle]
                held16[to, cut] = out[middle : start + size].astype(BF16)
            for j, (source, target) in enumerate(((held, mine), (held16, theirs))):
                copy = pltpu.make_async_copy(source.at[:, cut], target.at[:, cut], sem.at[k, j])
                copy.start()
                copies.append(copy)
        for copy in copies:
            copy.wait()

    return pl.pallas_call(
        body,
        in_specs=[VMEM] * (2 * len(pairs) + 2),
        out_specs=[VMEM] * 3 + [HBM] * 2,
        out_shape=[jax.ShapeDtypeStruct((rows, hidden), BF16)] * 3
        + [
            jax.ShapeDtypeStruct((half, features), F32),
            jax.ShapeDtypeStruct((half, features), BF16),
        ],
        scratch_shapes=[
            pltpu.VMEM((half, features), F32),
            pltpu.VMEM((half, features), BF16),
            pltpu.SemaphoreType.DMA((steps, 2)),
        ],
        cost_estimate=cost(4 * rows * hidden * features, 4 * hidden * features),
        compiler_params=pltpu.CompilerParams(vmem_limit_bytes=12 * MIB),
        name="backward",
    )(*[a for pair in pairs for a in pair], in_vmem(w_gate), in_vmem(w_up))


def piece_specs(pieces, per, tile):
    return [pl.BlockSpec((per, tile), lambda i, r=r: (r, i)) for _, r in pieces]


def weight_grads_in(xs, per, grad_gates, grad_ups):
    rows, features = per * len(xs), xs[0][0].shape[1]
    hidden = grad_gates[0].shape[1]
    tile = tile_of(features, 1024)
    n_x, n_g = len(xs), len(grad_gates)

    def body(*refs):
        x = jnp.concatenate([r[...] for r in refs[:n_x]], 0)
        gate = jnp.concatenate([r[...] for r in refs[n_x : n_x + n_g]], 0)
        up = jnp.concatenate([r[...] for r in refs[n_x + n_g : n_x + 2 * n_g]], 0)
        out_gate, out_up = refs[n_x + 2 * n_g :]
        out_gate[...] = dot_tn(x, gate).astype(BF16)
        out_up[...] = dot_tn(x, up).astype(BF16)

    whole = [pl.BlockSpec(g.shape, lambda i: (0, 0)) for g in grad_gates + grad_ups]
    out = pl.BlockSpec((tile, hidden), lambda i: (i, 0))
    return pl.pallas_call(
        body,
        grid=(features // tile,),
        in_specs=piece_specs(xs, per, tile) + whole,
        out_specs=[out, out],
        out_shape=[jax.ShapeDtypeStruct((features, hidden), BF16)] * 2,
        cost_estimate=cost(
            4 * rows * hidden * features, 4 * hidden * features + 2 * rows * features
        ),
        compiler_params=pltpu.CompilerParams(vmem_limit_bytes=40 * MIB),
        name="weight_grads_in",
    )(*[a for a, _ in xs], *grad_gates, *grad_ups)


def weight_grad_out(activations, dys, per):
    rows, features = per * len(dys), dys[0][0].shape[1]
    hidden = activations[0].shape[1]
    tile = tile_of(features, 1024)
    n_y, n_a = len(dys), len(activations)

    def body(*refs):
        out, turned = refs[n_y + n_a :]

        @pl.when(pl.program_id(0) == 0)
        def _():
            turned[...] = jnp.concatenate([r[...] for r in refs[n_y : n_y + n_a]], 0).T

        dy = jnp.concatenate([r[...] for r in refs[:n_y]], 0)
        out[...] = dot(turned[...], dy).astype(BF16)

    return pl.pallas_call(
        body,
        grid=(features // tile,),
        in_specs=piece_specs(dys, per, tile)
        + [pl.BlockSpec(a.shape, lambda i: (0, 0)) for a in activations],
        out_specs=pl.BlockSpec((hidden, tile), lambda i: (0, i)),
        out_shape=jax.ShapeDtypeStruct((hidden, features), BF16),
        scratch_shapes=[pltpu.VMEM((hidden, rows), BF16)],
        cost_estimate=cost(
            2 * rows * hidden * features, 2 * hidden * features + 2 * rows * features
        ),
        compiler_params=pltpu.CompilerParams(vmem_limit_bytes=40 * MIB),
        name="weight_grad_out",
    )(*[a for a, _ in dys], *activations)


def make_local(rows, cols):
    chips = rows // 2
    far = chips // 2
    order = list(range(0, chips, 2)) + list(range(1, chips, 2))[::-1]

    def shift(by):
        return [
            (2 * order[k] + core, 2 * order[(k + by) % chips] + core)
            for k in range(chips)
            for core in (0, 1)
        ]

    to_next, to_prev = shift(1), shift(-1)
    swap = [(i, i ^ 1) for i in range(rows)]

    def right(a):
        return lax.ppermute(a, "row", to_next)

    def left(a):
        return lax.ppermute(a, "row", to_prev)

    def sibling(a):
        return lax.ppermute(a, "row", swap)

    def others(rounded):
        got = [
            lax.ppermute(rounded, "col", [(i, (i + by) % cols) for i in range(cols)])
            for by in range(1, cols)
        ]
        if len(got) == 1:
            return got[0]
        return sum(g.astype(F32) for g in got)

    def local(tokens, cotangent, w_gate, w_up, w_down):
        per, features = tokens.shape
        at = {0: jnp.concatenate([tokens, cotangent], 0)}
        weights = load_weights(w_gate, w_up, w_down)
        groups = [[0]] + [[k, -k] for k in range(1, far)] + [[far]]
        xs, dys, grads, reduced = [], [], [], {}

        def go_forward(group):
            if group == [far]:
                x, dy = at[far]
                x, dy = [(x, 0), (sibling(x), 0)], [(dy, 0), (sibling(dy), 0)]
            else:
                blocks = [at[k] for k in group] + [sibling(at[k]) for k in group]
                x, dy = [(b, 0) for b in blocks], [(b, 1) for b in blocks]
            xs.extend(x)
            dys.extend(dy)
            own, rounded = forward(x, dy, per, *weights)
            return group, own, others(rounded)

        def go_backward(*waiting):
            *grad, mine, theirs = backward([w[1:] for w in waiting], *weights[:2])
            grads.append(grad)
            theirs = sibling(theirs)
            for i, k in enumerate(k for w in waiting for k in w[0]):
                cut = slice(i * per, (i + 1) * per)
                reduced[k] = (mine[cut], theirs[cut])
            return mine

        at[-1], at[1] = right(at[0]), left(at[0])
        waiting = go_forward(groups[0])
        done = [waiting[1]]
        for k in range(1, far):
            at[k], at[-k] = after((at[k], at[-k]), *done)
            if k + 1 < far:
                at[-k - 1], at[k + 1] = right(at[-k]), left(at[k])
            else:
                at[far] = right(at[-k][:per]), left(at[k][per:])
            latest = go_forward(groups[k])
            done = [latest[1]]
            if k + 1 < far:
                done.append(go_backward(waiting))
                waiting = latest
        at[far] = after(at[far], *done)
        last = go_forward(groups[far])
        own, other = after(waiting[1:], last[1])
        go_backward((waiting[0], own, other))
        go_backward(latest, last)

        half = features // 2
        outs = []
        for part in (0, 1):
            cut = slice(part * half, (part + 1) * half)

            def term(k):
                return reduced[k][0][:, cut] + reduced[k][1][:, cut].astype(F32)

            total = term(0)
            for send, sign in ((right, 1), (left, -1)):
                held = None
                if (sign > 0) == (part == 0):
                    held = send(term(far).astype(BF16)).astype(F32)
                for k in range(far - 1, 0, -1):
                    moved = term(sign * k)
                    moved = moved if held is None else moved + held
                    held = send(moved.astype(BF16)).astype(F32)
                if held is not None:
                    total = total + held
            outs.append(total)
        grad_tokens = jnp.concatenate(outs, 1).astype(BF16)

        gate_grads, up_grads, activations = ([g[i] for g in grads] for i in range(3))
        grad_w_gate, grad_w_up = weight_grads_in(xs, per, gate_grads, up_grads)
        grad_w_down = weight_grad_out(activations, dys, per)
        return grad_tokens, grad_w_gate, grad_w_up, grad_w_down

    return local


def solution(mesh):
    placed = (P("row", "col"), P("row", "col"), P("col", "row"), P("col", "row"), P("row", "col"))
    return jax.shard_map(
        make_local(mesh.shape["row"], mesh.shape["col"]),
        mesh=mesh,
        in_specs=placed,
        out_specs=(P("row", "col"), P("col", "row"), P("col", "row"), P("row", "col")),
        check_vma=False,
    )
```

```python
import jax
import jax.numpy as jnp
from jax import lax
from jax.experimental import pallas as pl
from jax.experimental.pallas import tpu as pltpu
from jax.sharding import PartitionSpec as P

F32, BF16 = jnp.float32, jnp.bfloat16
MIB = 2**20
NT = (((1,), (1,)), ((), ()))
TN = (((0,), (0,)), ((), ()))
HBM = pl.BlockSpec(memory_space=pl.ANY)
VMEM = pl.BlockSpec(memory_space=pltpu.VMEM)


def dot(left, right):
    return jnp.dot(left, right, preferred_element_type=F32)


def dot_nt(left, right):
    return lax.dot_general(left, right, NT, preferred_element_type=F32)


def dot_tn(left, right):
    return lax.dot_general(left, right, TN, preferred_element_type=F32)


def tile_of(size, most):
    return most if size % most == 0 else size


def after(values, *earlier):
    return lax.optimization_barrier((values, earlier))[0]


def in_vmem(a):
    return pltpu.with_memory_space_constraint(a, pltpu.VMEM)


def in_hbm(a):
    return pltpu.with_memory_space_constraint(a, pltpu.HBM)


def cost(flops, nbytes):
    return pl.CostEstimate(flops=flops, bytes_accessed=nbytes, transcendentals=0)


def load_weights(w_gate, w_up, w_down):
    features, hidden = w_gate.shape
    tile = tile_of(features, 1024)
    steps = features // tile

    def body(gate, up, down, out, piece, sem, piece_sem):
        whole = [
            pltpu.make_async_copy(source, out.at[:, pl.ds(j * hidden, hidden)], sem.at[j])
            for j, source in enumerate((gate, up))
        ]
        pieces = [
            pltpu.make_async_copy(
                down.at[:, pl.ds(i * tile, tile)], piece.at[i % 2], piece_sem.at[i]
            )
            for i in range(steps)
        ]
        pieces[0].start()
        for copy in whole:
            copy.start()
        for i in range(steps):
            if i + 1 < steps:
                pieces[i + 1].start()
            pieces[i].wait()
            out[pl.ds(i * tile, tile), pl.ds(2 * hidden, hidden)] = piece[i % 2].T
        for copy in whole:
            copy.wait()

    return pl.pallas_call(
        body,
        in_specs=[HBM] * 3,
        out_specs=VMEM,
        out_shape=pltpu.VMEM((features, 3 * hidden), BF16),
        scratch_shapes=[
            pltpu.VMEM((2, hidden, tile), BF16),
            pltpu.SemaphoreType.DMA((2,)),
            pltpu.SemaphoreType.DMA((steps,)),
        ],
        cost_estimate=cost(0, 6 * features * hidden),
        compiler_params=pltpu.CompilerParams(vmem_limit_bytes=8 * MIB),
        name="load_weights",
    )(in_hbm(w_gate), in_hbm(w_up), in_hbm(w_down))


def halves(first, second):
    rows, features = first.shape[0] // 2, first.shape[1]

    def body(one, two, upper, lower, sem):
        copies = [
            pltpu.make_async_copy(one.at[pl.ds(0, rows), :], upper, sem.at[0]),
            pltpu.make_async_copy(two.at[pl.ds(rows, rows), :], lower, sem.at[1]),
        ]
        for copy in copies:
            copy.start()
        for copy in copies:
            copy.wait()

    return pl.pallas_call(
        body,
        in_specs=[HBM] * 2,
        out_specs=[HBM] * 2,
        out_shape=[pltpu.HBM((rows, features), first.dtype)] * 2,
        scratch_shapes=[pltpu.SemaphoreType.DMA((2,))],
        cost_estimate=cost(0, 8 * rows * features),
        compiler_params=pltpu.CompilerParams(vmem_limit_bytes=1 * MIB),
        name="halves",
    )(first, second)


def forward(xs, dys, per, weights):
    features, hidden = weights.shape[0], weights.shape[1] // 3
    rows = per * len(xs)
    tile = tile_of(features, 2048)
    steps = features // tile
    arrays = []
    for a, _ in xs + dys:
        if not any(a is b for b in arrays):
            arrays.append(a)
    place = [([a is b for b in arrays].index(True), r) for a, r in xs + dys]
    count = len(arrays)

    def body(*refs):
        sources = refs[:count]
        weight, own, rounded, held, sem = refs[count:]
        copies = []
        for k in range(steps):
            cut = pl.ds(k * tile, tile)
            for i, (a, r) in enumerate(place):
                copy = pltpu.make_async_copy(
                    sources[a].at[pl.ds(r * per, per), cut],
                    held.at[pl.ds(i * per, per), cut],
                    sem.at[k, i],
                )
                copy.start()
                copies.append(copy)
        for k in range(steps):
            cut = pl.ds(k * tile, tile)
            for i in range(len(place)):
                copies[k * len(place) + i].wait()
            for j in range(3):
                out = pl.ds(j * hidden, hidden)
                source = pl.ds(rows if j == 2 else 0, rows)
                part = dot(held[source, cut], weight[cut, out])
                if k == 0:
                    own[:, out] = part
                else:
                    own[:, out] += part
        rounded[...] = own[...].astype(BF16)

    return pl.pallas_call(
        body,
        in_specs=[HBM] * count + [VMEM],
        out_specs=[VMEM] * 2,
        out_shape=[
            jax.ShapeDtypeStruct((rows, 3 * hidden), F32),
            jax.ShapeDtypeStruct((rows, 3 * hidden), BF16),
        ],
        scratch_shapes=[
            pltpu.VMEM((2 * rows, features), BF16),
            pltpu.SemaphoreType.DMA((steps, len(place))),
        ],
        cost_estimate=cost(6 * rows * hidden * features, 6 * hidden * features),
        compiler_params=pltpu.CompilerParams(vmem_limit_bytes=12 * MIB),
        name="forward",
    )(*arrays, in_vmem(weights))


def backward(pairs, weights):
    features, hidden = weights.shape[0], weights.shape[1] // 3
    sizes = [own.shape[0] for own, _ in pairs]
    rows = sum(sizes)
    half, tile = rows // 2, tile_of(features, 1024)
    steps = features // tile
    starts = [sum(sizes[:i]) for i in range(len(sizes))]

    def body(*refs):
        sums, refs = refs[: 2 * len(pairs)], refs[2 * len(pairs) :]
        weight, gate_to, up_to, act_to, mine, theirs = refs[:6]
        gate_out, up_out, act_out, held, held16, sem, out_sem = refs[6:]
        for i, size in enumerate(sizes):
            own, other, at = sums[2 * i], sums[2 * i + 1], pl.ds(starts[i], size)

            def total(j, own=own, other=other):
                cut = pl.ds(j * hidden, hidden)
                return own[:, cut] + other[:, cut].astype(F32)

            gate_value, up_value, grad_act = total(0), total(1), total(2)
            sigmoid_gate = jax.nn.sigmoid(gate_value)
            silu_gate = gate_value * sigmoid_gate
            act_out[at, :] = (silu_gate * up_value).astype(BF16)
            up_out[at, :] = (grad_act * silu_gate).astype(BF16)
            gate_out[at, :] = (
                grad_act * up_value * sigmoid_gate * (1.0 + gate_value * (1.0 - sigmoid_gate))
            ).astype(BF16)
        copies = [
            pltpu.make_async_copy(source, target, out_sem.at[j])
            for j, (source, target) in enumerate(
                ((gate_out, gate_to), (up_out, up_to), (act_out, act_to))
            )
        ]
        for copy in copies:
            copy.start()
        for k in range(steps):
            cut = pl.ds(k * tile, tile)
            out = dot_nt(gate_out[...], weight[cut, pl.ds(0, hidden)])
            out += dot_nt(up_out[...], weight[cut, pl.ds(hidden, hidden)])
            for start, size in zip(starts, sizes):
                to, middle = pl.ds(start // 2, size // 2), start + size // 2
                held[to, cut] = out[start:middle]
                held16[to, cut] = out[middle : start + size].astype(BF16)
            for j, (source, target) in enumerate(((held, mine), (held16, theirs))):
                copy = pltpu.make_async_copy(source.at[:, cut], target.at[:, cut], sem.at[k, j])
                copy.start()
                copies.append(copy)
        for copy in copies:
            copy.wait()

    return pl.pallas_call(
        body,
        in_specs=[VMEM] * (2 * len(pairs) + 1),
        out_specs=[HBM] * 5,
        out_shape=[pltpu.HBM((rows, hidden), BF16)] * 3
        + [pltpu.HBM((half, features), F32), pltpu.HBM((half, features), BF16)],
        scratch_shapes=[pltpu.VMEM((rows, hidden), BF16)] * 3
        + [
            pltpu.VMEM((half, features), F32),
            pltpu.VMEM((half, features), BF16),
            pltpu.SemaphoreType.DMA((steps, 2)),
            pltpu.SemaphoreType.DMA((3,)),
        ],
        cost_estimate=cost(4 * rows * hidden * features, 4 * hidden * features),
        compiler_params=pltpu.CompilerParams(vmem_limit_bytes=12 * MIB),
        name="backward",
    )(*[a for pair in pairs for a in pair], in_vmem(weights))


PARTS = 2


def part_of(part, features, most):
    tile = tile_of(features // PARTS, most)
    steps = features // PARTS // tile
    return tile, steps, part * steps


def piece_specs(pieces, per, tile, first):
    return [pl.BlockSpec((per, tile), lambda i, r=r: (r, first + i)) for _, r in pieces]


def weight_grads_in(xs, per, grad_gates, grad_ups, part, before):
    rows, features = per * len(xs), xs[0][0].shape[1]
    hidden = grad_gates[0].shape[1]
    tile, steps, first = part_of(part, features, 1024)
    n_x, n_g = len(xs), len(grad_gates)

    def body(*refs):
        x = jnp.concatenate([r[...] for r in refs[:n_x]], 0)
        gate = jnp.concatenate([r[...] for r in refs[n_x : n_x + n_g]], 0)
        up = jnp.concatenate([r[...] for r in refs[n_x + n_g : n_x + 2 * n_g]], 0)
        out_gate, out_up = refs[-2:]
        out_gate[...] = dot_tn(x, gate).astype(BF16)
        out_up[...] = dot_tn(x, up).astype(BF16)

    whole = [pl.BlockSpec(g.shape, lambda i: (0, 0)) for g in grad_gates + grad_ups]
    out = pl.BlockSpec((tile, hidden), lambda i: (first + i, 0))
    given = [a for a, _ in xs] + grad_gates + grad_ups
    return pl.pallas_call(
        body,
        grid=(steps,),
        in_specs=piece_specs(xs, per, tile, first) + whole + [HBM] * len(before),
        out_specs=[out, out],
        out_shape=[jax.ShapeDtypeStruct((features, hidden), BF16)] * 2,
        input_output_aliases={len(given) + j: j for j in range(len(before))},
        cost_estimate=cost(
            4 * rows * hidden * features // PARTS,
            (4 * hidden * features + 2 * rows * features) // PARTS,
        ),
        compiler_params=pltpu.CompilerParams(vmem_limit_bytes=40 * MIB),
        name="weight_grads_in",
    )(*[in_hbm(a) for a in given], *before)


def weight_grad_out(activations, dys, per, part, before):
    rows, features = per * len(dys), dys[0][0].shape[1]
    hidden = activations[0].shape[1]
    tile, steps, first = part_of(part, features, 1024)
    n_y, n_a = len(dys), len(activations)

    def body(*refs):
        out, turned = refs[-2:]

        @pl.when(pl.program_id(0) == 0)
        def _():
            turned[...] = jnp.concatenate([r[...] for r in refs[n_y : n_y + n_a]], 0).T

        dy = jnp.concatenate([r[...] for r in refs[:n_y]], 0)
        out[...] = dot(turned[...], dy).astype(BF16)

    given = [a for a, _ in dys] + activations
    return pl.pallas_call(
        body,
        grid=(steps,),
        in_specs=piece_specs(dys, per, tile, first)
        + [pl.BlockSpec(a.shape, lambda i: (0, 0)) for a in activations]
        + [HBM] * len(before),
        out_specs=[pl.BlockSpec((hidden, tile), lambda i: (0, first + i))],
        out_shape=[jax.ShapeDtypeStruct((hidden, features), BF16)],
        input_output_aliases={len(given) + j: j for j in range(len(before))},
        scratch_shapes=[pltpu.VMEM((hidden, rows), BF16)],
        cost_estimate=cost(
            2 * rows * hidden * features // PARTS,
            (2 * hidden * features + 2 * rows * features) // PARTS,
        ),
        compiler_params=pltpu.CompilerParams(vmem_limit_bytes=40 * MIB),
        name="weight_grad_out",
    )(*[in_hbm(a) for a in given], *before)


def add_up(outs, rows, width):
    columns = [column for out in outs for column in out]
    given = [block for column in columns for block in column]
    tile = tile_of(width, 2048)
    steps = width // tile

    def body(*refs):
        sources, targets = list(refs[: len(given)]), refs[len(given) : len(given) + len(outs)]
        held, sem = refs[-2:]
        step = pl.program_id(0)
        at, copies = 0, []
        for target, out in zip(targets, outs):
            for j, column in enumerate(out):
                total = sources.pop(0)[...].astype(F32)
                for _ in column[1:]:
                    total = total + sources.pop(0)[...].astype(F32)
                held[at] = total.astype(BF16)
                cut = pl.ds(pl.multiple_of(j * width + step * tile, tile), tile)
                copies.append(pltpu.make_async_copy(held.at[at], target.at[:, cut], sem.at[at]))
                copies[-1].start()
                at += 1
        for copy in copies:
            copy.wait()

    return pl.pallas_call(
        body,
        grid=(steps,),
        in_specs=[
            pl.BlockSpec((rows, tile), lambda i, r=r, c=c: (r, c * steps + i)) for _, r, c in given
        ],
        out_specs=[HBM] * len(outs),
        out_shape=[jax.ShapeDtypeStruct((rows, len(out) * width), BF16) for out in outs],
        scratch_shapes=[
            pltpu.VMEM((len(columns), rows, tile), BF16),
            pltpu.SemaphoreType.DMA((len(columns),)),
        ],
        cost_estimate=cost(0, 4 * rows * width * len(given)),
        compiler_params=pltpu.CompilerParams(vmem_limit_bytes=24 * MIB),
        name="add_up",
    )(*[in_hbm(a) if a.dtype == F32 else a for a, _, _ in given])


def make_local(rows, cols):
    chips = rows // 2
    far = chips // 2
    order = list(range(0, chips, 2)) + list(range(1, chips, 2))[::-1]

    def shift(by):
        return [
            (2 * order[k] + core, 2 * order[(k + by) % chips] + core)
            for k in range(chips)
            for core in (0, 1)
        ]

    to_next, to_prev = shift(1), shift(-1)
    swap = [(i, i ^ 1) for i in range(rows)]

    def right(a):
        return lax.ppermute(a, "row", to_next)

    def left(a):
        return lax.ppermute(a, "row", to_prev)

    def sibling(a):
        return lax.ppermute(a, "row", swap)

    def others(rounded):
        got = [
            lax.ppermute(rounded, "col", [(i, (i + by) % cols) for i in range(cols)])
            for by in range(1, cols)
        ]
        if len(got) == 1:
            return got[0]
        return sum(g.astype(F32) for g in got)

    def local(tokens, cotangent, w_gate, w_up, w_down):
        per, features = tokens.shape
        at = {0: jnp.concatenate([tokens, cotangent], 0)}
        weights = load_weights(w_gate, w_up, w_down)
        groups = [[0]] + [[k, -k] for k in range(1, far)] + [[far]]
        xs, dys, grads, reduced = [], [], [], {}

        def go_forward(group):
            if group == [far]:
                x, dy = at[far]
                x, dy = [(x, 0), (sibling(x), 0)], [(dy, 0), (sibling(dy), 0)]
            else:
                blocks = [at[k] for k in group] + [sibling(at[k]) for k in group]
                x, dy = [(b, 0) for b in blocks], [(b, 1) for b in blocks]
            xs.extend(x)
            dys.extend(dy)
            own, rounded = forward(x, dy, per, weights)
            return group, own, others(rounded)

        def go_backward(*waiting):
            *grad, mine, theirs = backward([w[1:] for w in waiting], weights)
            grads.append(grad)
            theirs = sibling(theirs)
            for i, k in enumerate(k for w in waiting for k in w[0]):
                reduced[k] = [(mine, i), (theirs, i)]
            return mine

        at[-1], at[1] = right(at[0]), left(at[0])
        waiting = go_forward(groups[0])
        done = [waiting[1]]
        for k in range(1, far):
            at[k], at[-k] = after((at[k], at[-k]), *done)
            if k + 1 < far:
                at[-k - 1], at[k + 1] = right(at[-k]), left(at[k])
            else:
                x, dy = halves(at[-k], at[k])
                at[far] = right(x), left(dy)
            latest = go_forward(groups[k])
            done = [latest[1]]
            if k + 2 == far:
                done.append(latest[2])
            if k + 1 < far:
                done.append(go_backward((waiting[0], *after(waiting[1:], latest[1]))))
                waiting = latest
        at[far] = after(at[far], *done)
        last = go_forward(groups[far])
        done = go_backward((waiting[0], *after(waiting[1:], last[1])))
        go_backward((latest[0], *after(latest[1:], done)), last)

        gate_grads, up_grads, activations = ([g[i] for g in grads] for i in range(3))
        parts = [(kind, part) for kind in ("in", "out") for part in range(PARTS)]
        made = {"in": [], "out": []}

        def term(k, half):
            return [(a, i, half) for a, i in reduced[k]]

        came = None
        for hop in range(far):
            near = far - hop
            behind = far if hop == 0 else -near
            going = [[term(near, 0)], [term(behind, 1)]]
            if near > 1:
                going = [going[0] + [term(near - 1, 1)], [term(1 - near, 0)] + going[1]]
            if came is not None:
                going[0][0] = going[0][0] + [(came[0], 0, 0)]
                going[1][-1] = going[1][-1] + [(came[1], 0, 1)]
                if near > 1:
                    going[0][1] = going[0][1] + [(came[0], 0, 1)]
                    going[1][0] = going[1][0] + [(came[1], 0, 0)]
            going = add_up(going, per, features // 2)
            if hop:
                going, made = lax.optimization_barrier((going, made))
            before, came = came, (right(going[0]), left(going[1]))
            for kind, part in parts[:1]:
                if kind == "in":
                    made[kind] = weight_grads_in(xs, per, gate_grads, up_grads, part, made[kind])
                else:
                    made[kind] = weight_grad_out(activations, dys, per, part, made[kind])
            parts = parts[1:]
        for kind, part in parts:
            made[kind] = weight_grad_out(activations, dys, per, part, made[kind])
        last = [
            term(0, 0) + [(came[0], 0, 0), (before[1], 0, 0)],
            term(0, 1) + [(came[1], 0, 0), (before[0], 0, 1)],
        ]
        (grad_tokens,) = add_up([last], per, features // 2)
        return (grad_tokens, *made["in"], *made["out"])

    return local


def solution(mesh):
    placed = (P("row", "col"), P("row", "col"), P("col", "row"), P("col", "row"), P("row", "col"))
    return jax.shard_map(
        make_local(mesh.shape["row"], mesh.shape["col"]),
        mesh=mesh,
        in_specs=placed,
        out_specs=(P("row", "col"), P("col", "row"), P("col", "row"), P("row", "col")),
        check_vma=False,
    )
```

```python
import jax
import jax.numpy as jnp
from jax import lax
from jax.experimental import pallas as pl
from jax.experimental.pallas import tpu as pltpu
from jax.sharding import PartitionSpec as P

F32, BF16 = jnp.float32, jnp.bfloat16
MIB = 2**20
NT = (((1,), (1,)), ((), ()))
TN = (((0,), (0,)), ((), ()))
HBM = pl.BlockSpec(memory_space=pl.ANY)
VMEM = pl.BlockSpec(memory_space=pltpu.VMEM)


def dot(left, right):
    return jnp.dot(left, right, preferred_element_type=F32)


def dot_nt(left, right):
    return lax.dot_general(left, right, NT, preferred_element_type=F32)


def dot_tn(left, right):
    return lax.dot_general(left, right, TN, preferred_element_type=F32)


def tile_of(size, most):
    return most if size % most == 0 else size


def after(values, *earlier):
    return lax.optimization_barrier((values, earlier))[0]


def in_vmem(a):
    return pltpu.with_memory_space_constraint(a, pltpu.VMEM)


def in_hbm(a):
    return pltpu.with_memory_space_constraint(a, pltpu.HBM)


def cost(flops, nbytes):
    return pl.CostEstimate(flops=flops, bytes_accessed=nbytes, transcendentals=0)


def load_weights(w_gate, w_up, w_down):
    features, hidden = w_gate.shape
    tile = tile_of(features, 1024)
    steps = features // tile

    def body(gate, up, down, out, piece, sem, piece_sem):
        whole = [
            pltpu.make_async_copy(source, out.at[:, pl.ds(j * hidden, hidden)], sem.at[j])
            for j, source in enumerate((gate, up))
        ]
        pieces = [
            pltpu.make_async_copy(
                down.at[:, pl.ds(i * tile, tile)], piece.at[i % 2], piece_sem.at[i]
            )
            for i in range(steps)
        ]
        pieces[0].start()
        for copy in whole:
            copy.start()
        for i in range(steps):
            if i + 1 < steps:
                pieces[i + 1].start()
            pieces[i].wait()
            out[pl.ds(i * tile, tile), pl.ds(2 * hidden, hidden)] = piece[i % 2].T
        for copy in whole:
            copy.wait()

    return pl.pallas_call(
        body,
        in_specs=[HBM] * 3,
        out_specs=VMEM,
        out_shape=pltpu.VMEM((features, 3 * hidden), BF16),
        scratch_shapes=[
            pltpu.VMEM((2, hidden, tile), BF16),
            pltpu.SemaphoreType.DMA((2,)),
            pltpu.SemaphoreType.DMA((steps,)),
        ],
        cost_estimate=cost(0, 6 * features * hidden),
        compiler_params=pltpu.CompilerParams(vmem_limit_bytes=8 * MIB),
        name="load_weights",
    )(in_hbm(w_gate), in_hbm(w_up), in_hbm(w_down))


def small_copies(sources, out_shapes):
    arrays = [a for out in sources for a, _ in out]

    def body(*refs):
        given, outs, sem = list(refs[: len(arrays)]), refs[len(arrays) : -1], refs[-1]
        copies = []
        for out, blocks, (rows, _) in zip(outs, sources, out_shapes):
            rows //= len(blocks)
            for i, (_, first) in enumerate(blocks):
                copies.append(
                    pltpu.make_async_copy(
                        given.pop(0).at[pl.ds(first, rows), :],
                        out.at[pl.ds(i * rows, rows), :],
                        sem.at[len(copies)],
                    )
                )
        for copy in copies:
            copy.start()
        for copy in copies:
            copy.wait()

    return pl.pallas_call(
        body,
        in_specs=[HBM] * len(arrays),
        out_specs=[HBM] * len(out_shapes),
        out_shape=[pltpu.HBM(shape, BF16) for shape in out_shapes],
        scratch_shapes=[pltpu.SemaphoreType.DMA((len(arrays),))],
        cost_estimate=cost(0, 4 * sum(r * f for r, f in out_shapes)),
        compiler_params=pltpu.CompilerParams(vmem_limit_bytes=MIB),
        name="small_copies",
    )(*arrays)


def forward(xs, dys, per, weights):
    features, hidden = weights.shape[0], weights.shape[1] // 3
    rows = per * len(xs)
    tile = tile_of(features, 2048)
    steps = features // tile
    arrays = []
    for a, _ in xs + dys:
        if not any(a is b for b in arrays):
            arrays.append(a)
    place = [([a is b for b in arrays].index(True), r) for a, r in xs + dys]
    count = len(arrays)

    def body(*refs):
        sources = refs[:count]
        weight, own, rounded, held, sem = refs[count:]
        copies = []
        for k in range(steps):
            cut = pl.ds(k * tile, tile)
            for i, (a, r) in enumerate(place):
                copy = pltpu.make_async_copy(
                    sources[a].at[pl.ds(r * per, per), cut],
                    held.at[pl.ds(i * per, per), cut],
                    sem.at[k, i],
                )
                copy.start()
                copies.append(copy)
        for k in range(steps):
            cut = pl.ds(k * tile, tile)
            for i in range(len(place)):
                copies[k * len(place) + i].wait()
            for j in range(3):
                out = pl.ds(j * hidden, hidden)
                source = pl.ds(rows if j == 2 else 0, rows)
                part = dot(held[source, cut], weight[cut, out])
                if k == 0:
                    own[:, out] = part
                else:
                    own[:, out] += part
        rounded[...] = own[...].astype(BF16)

    return pl.pallas_call(
        body,
        in_specs=[HBM] * count + [VMEM],
        out_specs=[VMEM] * 2,
        out_shape=[
            jax.ShapeDtypeStruct((rows, 3 * hidden), F32),
            jax.ShapeDtypeStruct((rows, 3 * hidden), BF16),
        ],
        scratch_shapes=[
            pltpu.VMEM((2 * rows, features), BF16),
            pltpu.SemaphoreType.DMA((steps, len(place))),
        ],
        cost_estimate=cost(6 * rows * hidden * features, 6 * hidden * features),
        compiler_params=pltpu.CompilerParams(vmem_limit_bytes=12 * MIB),
        name="forward",
    )(*arrays, in_vmem(weights))


def backward(pairs, weights):
    features, hidden = weights.shape[0], weights.shape[1] // 3
    sizes = [own.shape[0] for own, _ in pairs]
    rows = sum(sizes)
    half, tile = rows // 2, tile_of(features, 1024)
    steps = features // tile
    padded = -(-rows // 128) * 128
    starts = [sum(sizes[:i]) for i in range(len(sizes))]

    def body(*refs):
        sums, refs = refs[: 2 * len(pairs)], refs[2 * len(pairs) :]
        weight, gate_to, up_to, act_to, mine, theirs = refs[:6]
        gate_out, up_out, act_out, turned, held, held16, sem, out_sem = refs[6:]
        for i, size in enumerate(sizes):
            own, other, at = sums[2 * i], sums[2 * i + 1], pl.ds(starts[i], size)

            def total(j, own=own, other=other):
                cut = pl.ds(j * hidden, hidden)
                return own[:, cut] + other[:, cut].astype(F32)

            gate_value, up_value, grad_act = total(0), total(1), total(2)
            sigmoid_gate = jax.nn.sigmoid(gate_value)
            silu_gate = gate_value * sigmoid_gate
            act_out[at, :] = (silu_gate * up_value).astype(BF16)
            up_out[at, :] = (grad_act * silu_gate).astype(BF16)
            gate_out[at, :] = (
                grad_act * up_value * sigmoid_gate * (1.0 + gate_value * (1.0 - sigmoid_gate))
            ).astype(BF16)
        copies = [
            pltpu.make_async_copy(source, target, out_sem.at[j])
            for j, (source, target) in enumerate(
                ((gate_out, gate_to), (up_out, up_to), (act_out, act_to))
            )
        ]
        for copy in copies:
            copy.start()
        if padded > rows:
            turned[:, rows:] = jnp.zeros((2 * hidden, padded - rows), BF16)
        turned[:hidden, :rows] = gate_out[...].T
        turned[hidden:, :rows] = up_out[...].T
        for k in range(steps):
            cut = pl.ds(k * tile, tile)
            out = dot(weight[cut, pl.ds(0, 2 * hidden)], turned[...]).T
            for start, size in zip(starts, sizes):
                to, middle = pl.ds(start // 2, size // 2), start + size // 2
                held[to, cut] = out[start:middle]
                held16[to, cut] = out[middle : start + size].astype(BF16)
            for j, (source, target) in enumerate(((held, mine), (held16, theirs))):
                copy = pltpu.make_async_copy(source.at[:, cut], target.at[:, cut], sem.at[k, j])
                copy.start()
                copies.append(copy)
        for copy in copies:
            copy.wait()

    return pl.pallas_call(
        body,
        in_specs=[VMEM] * (2 * len(pairs) + 1),
        out_specs=[HBM] * 5,
        out_shape=[pltpu.HBM((rows, hidden), BF16)] * 3
        + [pltpu.HBM((half, features), F32), pltpu.HBM((half, features), BF16)],
        scratch_shapes=[pltpu.VMEM((rows, hidden), BF16)] * 3
        + [
            pltpu.VMEM((2 * hidden, padded), BF16),
            pltpu.VMEM((half, features), F32),
            pltpu.VMEM((half, features), BF16),
            pltpu.SemaphoreType.DMA((steps, 2)),
            pltpu.SemaphoreType.DMA((3,)),
        ],
        cost_estimate=cost(4 * rows * hidden * features, 4 * hidden * features),
        compiler_params=pltpu.CompilerParams(vmem_limit_bytes=12 * MIB),
        name="backward",
    )(*[a for pair in pairs for a in pair], in_vmem(weights))


PARTS = 2


def part_of(part, features, most):
    tile = tile_of(features // PARTS, most)
    steps = features // PARTS // tile
    return tile, steps, part * steps


def piece_specs(pieces, per, tile, first):
    return [pl.BlockSpec((per, tile), lambda i, r=r: (r, first + i)) for _, r in pieces]


def weight_grads_in(xs, per, grad_gates, grad_ups, part, before):
    rows, features = per * len(xs), xs[0][0].shape[1]
    hidden = grad_gates[0].shape[1]
    tile, steps, first = part_of(part, features, 1024)
    n_x, n_g = len(xs), len(grad_gates)

    def body(*refs):
        x = jnp.concatenate([r[...] for r in refs[:n_x]], 0)
        gate = jnp.concatenate([r[...] for r in refs[n_x : n_x + n_g]], 0)
        up = jnp.concatenate([r[...] for r in refs[n_x + n_g : n_x + 2 * n_g]], 0)
        out_gate, out_up = refs[-2:]
        out_gate[...] = dot_tn(x, gate).astype(BF16)
        out_up[...] = dot_tn(x, up).astype(BF16)

    whole = [pl.BlockSpec(g.shape, lambda i: (0, 0)) for g in grad_gates + grad_ups]
    out = pl.BlockSpec((tile, hidden), lambda i: (first + i, 0))
    given = [a for a, _ in xs] + grad_gates + grad_ups
    return pl.pallas_call(
        body,
        grid=(steps,),
        in_specs=piece_specs(xs, per, tile, first) + whole + [HBM] * len(before),
        out_specs=[out, out],
        out_shape=[jax.ShapeDtypeStruct((features, hidden), BF16)] * 2,
        input_output_aliases={len(given) + j: j for j in range(len(before))},
        cost_estimate=cost(
            4 * rows * hidden * features // PARTS,
            (4 * hidden * features + 2 * rows * features) // PARTS,
        ),
        compiler_params=pltpu.CompilerParams(vmem_limit_bytes=40 * MIB),
        name="weight_grads_in",
    )(*[in_hbm(a) for a in given], *before)


def weight_grad_out(activations, dys, per, part, before):
    rows, features = per * len(dys), dys[0][0].shape[1]
    hidden = activations[0].shape[1]
    tile, steps, first = part_of(part, features, 1024)
    n_y, n_a = len(dys), len(activations)

    def body(*refs):
        out, turned = refs[-2:]

        @pl.when(pl.program_id(0) == 0)
        def _():
            turned[...] = jnp.concatenate([r[...] for r in refs[n_y : n_y + n_a]], 0).T

        dy = jnp.concatenate([r[...] for r in refs[:n_y]], 0)
        out[...] = dot(turned[...], dy).astype(BF16)

    given = [a for a, _ in dys] + activations
    return pl.pallas_call(
        body,
        grid=(steps,),
        in_specs=piece_specs(dys, per, tile, first)
        + [pl.BlockSpec(a.shape, lambda i: (0, 0)) for a in activations]
        + [HBM] * len(before),
        out_specs=[pl.BlockSpec((hidden, tile), lambda i: (0, first + i))],
        out_shape=[jax.ShapeDtypeStruct((hidden, features), BF16)],
        input_output_aliases={len(given) + j: j for j in range(len(before))},
        scratch_shapes=[pltpu.VMEM((hidden, rows), BF16)],
        cost_estimate=cost(
            2 * rows * hidden * features // PARTS,
            (2 * hidden * features + 2 * rows * features) // PARTS,
        ),
        compiler_params=pltpu.CompilerParams(vmem_limit_bytes=40 * MIB),
        name="weight_grad_out",
    )(*[in_hbm(a) for a in given], *before)


def add_up(outs, rows, width):
    columns = [column for out in outs for column in out]
    given = [block for column in columns for block in column]
    tile = tile_of(width, 4096)
    steps = width // tile

    def body(*refs):
        sources, targets = list(refs[: len(given)]), refs[len(given) : len(given) + len(outs)]
        held, sem = refs[-2:]
        step = pl.program_id(0)
        at, copies = 0, []
        for target, out in zip(targets, outs):
            for j, column in enumerate(out):
                total = sources.pop(0)[...].astype(F32)
                for _ in column[1:]:
                    total = total + sources.pop(0)[...].astype(F32)
                held[at] = total.astype(BF16)
                cut = pl.ds(pl.multiple_of(j * width + step * tile, tile), tile)
                copies.append(pltpu.make_async_copy(held.at[at], target.at[:, cut], sem.at[at]))
                copies[-1].start()
                at += 1
        for copy in copies:
            copy.wait()

    return pl.pallas_call(
        body,
        grid=(steps,),
        in_specs=[
            pl.BlockSpec((rows, tile), lambda i, r=r, c=c: (r, c * steps + i)) for _, r, c in given
        ],
        out_specs=[HBM] * len(outs),
        out_shape=[jax.ShapeDtypeStruct((rows, len(out) * width), BF16) for out in outs],
        scratch_shapes=[
            pltpu.VMEM((len(columns), rows, tile), BF16),
            pltpu.SemaphoreType.DMA((len(columns),)),
        ],
        cost_estimate=cost(0, 4 * rows * width * len(given)),
        compiler_params=pltpu.CompilerParams(vmem_limit_bytes=24 * MIB),
        name="add_up",
    )(*[in_hbm(a) if a.dtype == F32 else a for a, _, _ in given])


def make_local(rows, cols):
    chips = rows // 2
    far = chips // 2
    order = list(range(0, chips, 2)) + list(range(1, chips, 2))[::-1]

    def shift(by):
        return [
            (2 * order[k] + core, 2 * order[(k + by) % chips] + core)
            for k in range(chips)
            for core in (0, 1)
        ]

    to_next, to_prev = shift(1), shift(-1)
    swap = [(i, i ^ 1) for i in range(rows)]

    def right(a):
        return lax.ppermute(a, "row", to_next)

    def left(a):
        return lax.ppermute(a, "row", to_prev)

    def sibling(a):
        return lax.ppermute(a, "row", swap)

    def others(rounded):
        got = [
            lax.ppermute(rounded, "col", [(i, (i + by) % cols) for i in range(cols)])
            for by in range(1, cols)
        ]
        if len(got) == 1:
            return got[0]
        return sum(g.astype(F32) for g in got)

    def local(tokens, cotangent, w_gate, w_up, w_down):
        per, features = tokens.shape
        at = {0: jnp.concatenate([tokens, cotangent], 0)}
        weights = load_weights(w_gate, w_up, w_down)
        groups = [[0]] + [[k, -k] for k in range(1, far)] + [[far]]
        xs, dys, grads, reduced = [], [], [], {}

        def go_forward(group):
            if group == [far]:
                x, dy = at[far]
                x, dy = [(x, 0), (sibling(x), 0)], [(dy, 0), (sibling(dy), 0)]
            else:
                blocks = [at[k] for k in group] + [sibling(at[k]) for k in group]
                x, dy = [(b, 0) for b in blocks], [(b, 1) for b in blocks]
            xs.extend(x)
            dys.extend(dy)
            own, rounded = forward(x, dy, per, weights)
            if group not in (groups[0], groups[far]):
                rounded = after(rounded, latest[2])
            return group, own, others(rounded)

        def go_backward(*waiting):
            *grad, mine, theirs = backward([w[1:] for w in waiting], weights)
            grads.append(grad)
            theirs = sibling(theirs)
            for i, k in enumerate(k for w in waiting for k in w[0]):
                reduced[k] = [(mine, i), (theirs, i)]
            return mine

        at[-1], at[1] = right(at[0]), left(at[0])
        waiting = latest = go_forward(groups[0])
        done = [waiting[1]]
        for k in range(1, far):
            at[k], at[-k] = after((at[k], at[-k]), *done)
            if k + 1 < far:
                at[-k - 1], at[k + 1] = right(at[-k]), left(at[k])
            else:
                x, dy = small_copies([[(at[-k], 0)], [(at[k], per)]], [tokens.shape] * 2)
                at[far] = right(x), left(dy)
            latest = go_forward(groups[k])
            done = [latest[1]]
            if k + 1 < far:
                done.append(latest[2])
                done.append(go_backward((waiting[0], *after(waiting[1:], latest[1]))))
                waiting = latest
        at[far] = after(at[far], *done)
        last = go_forward(groups[far])
        done = go_backward((waiting[0], *after(waiting[1:], last[1])))
        go_backward((latest[0], *after(latest[1:], done)), last)

        gate_grads, up_grads, activations = ([g[i] for g in grads] for i in range(3))
        parts = [(kind, part) for kind in ("in", "out") for part in range(PARTS)]
        made = {"in": [], "out": []}

        def term(k, half):
            return [(a, i, half) for a, i in reduced[k]]

        came = None
        for hop in range(far):
            near = far - hop
            behind = far if hop == 0 else -near
            going = [[term(near, 0)], [term(behind, 1)]]
            if near > 1:
                going = [going[0] + [term(near - 1, 1)], [term(1 - near, 0)] + going[1]]
            if came is not None:
                going[0][0] = going[0][0] + [(came[0], 0, 0)]
                going[1][-1] = going[1][-1] + [(came[1], 0, 1)]
                if near > 1:
                    going[0][1] = going[0][1] + [(came[0], 0, 1)]
                    going[1][0] = going[1][0] + [(came[1], 0, 0)]
            going = add_up(going, per, features // 2)
            if hop:
                going, made = lax.optimization_barrier((going, made))
            before, came = came, (right(going[0]), left(going[1]))
            for kind, part in parts[:1]:
                if kind == "in":
                    made[kind] = weight_grads_in(xs, per, gate_grads, up_grads, part, made[kind])
                else:
                    made[kind] = weight_grad_out(activations, dys, per, part, made[kind])
            parts = parts[1:]
        for kind, part in parts:
            made[kind] = weight_grad_out(activations, dys, per, part, made[kind])
        last = [
            term(0, 0) + [(came[0], 0, 0), (before[1], 0, 0)],
            term(0, 1) + [(came[1], 0, 0), (before[0], 0, 1)],
        ]
        (grad_tokens,) = add_up([last], per, features // 2)
        return (grad_tokens, *made["in"], *made["out"])

    return local


def solution(mesh):
    placed = (P("row", "col"), P("row", "col"), P("col", "row"), P("col", "row"), P("row", "col"))
    return jax.shard_map(
        make_local(mesh.shape["row"], mesh.shape["col"]),
        mesh=mesh,
        in_specs=placed,
        out_specs=(P("row", "col"), P("col", "row"), P("col", "row"), P("row", "col")),
        check_vma=False,
    )
```

```python
import math

import jax
import jax.numpy as jnp
from jax import lax
from jax.experimental import pallas as pl
from jax.experimental.pallas import tpu as pltpu
from jax.sharding import PartitionSpec as P

F32, BF16 = jnp.float32, jnp.bfloat16
MIB = 2**20
NT = (((1,), (1,)), ((), ()))
TN = (((0,), (0,)), ((), ()))
HBM = pl.BlockSpec(memory_space=pl.ANY)
VMEM = pl.BlockSpec(memory_space=pltpu.VMEM)


def dot(left, right):
    return jnp.dot(left, right, preferred_element_type=F32)


def dot_nt(left, right):
    return lax.dot_general(left, right, NT, preferred_element_type=F32)


def dot_tn(left, right):
    return lax.dot_general(left, right, TN, preferred_element_type=F32)


def tile_of(size, most):
    return most if size % most == 0 else size


def after(values, *earlier):
    return lax.optimization_barrier((values, earlier))[0]


def in_vmem(a):
    return pltpu.with_memory_space_constraint(a, pltpu.VMEM)


def in_hbm(a):
    return pltpu.with_memory_space_constraint(a, pltpu.HBM)


def cost(flops, nbytes):
    return pl.CostEstimate(flops=flops, bytes_accessed=nbytes, transcendentals=0)


def load_weights(w_gate, w_up, w_down):
    features, hidden = w_gate.shape
    tile = tile_of(features, 1024)
    steps = features // tile

    def body(gate, up, down, out, piece, sem, piece_sem):
        whole = [
            pltpu.make_async_copy(source, out.at[:, pl.ds(j * hidden, hidden)], sem.at[j])
            for j, source in enumerate((gate, up))
        ]
        pieces = [
            pltpu.make_async_copy(
                down.at[:, pl.ds(i * tile, tile)], piece.at[i % 2], piece_sem.at[i]
            )
            for i in range(steps)
        ]
        pieces[0].start()
        for copy in whole:
            copy.start()
        for i in range(steps):
            if i + 1 < steps:
                pieces[i + 1].start()
            pieces[i].wait()
            out[pl.ds(i * tile, tile), pl.ds(2 * hidden, hidden)] = piece[i % 2].T
        for copy in whole:
            copy.wait()

    return pl.pallas_call(
        body,
        in_specs=[HBM] * 3,
        out_specs=VMEM,
        out_shape=pltpu.VMEM((features, 3 * hidden), BF16),
        scratch_shapes=[
            pltpu.VMEM((2, hidden, tile), BF16),
            pltpu.SemaphoreType.DMA((2,)),
            pltpu.SemaphoreType.DMA((steps,)),
        ],
        cost_estimate=cost(0, 6 * features * hidden),
        compiler_params=pltpu.CompilerParams(vmem_limit_bytes=8 * MIB),
        name="load_weights",
    )(in_hbm(w_gate), in_hbm(w_up), in_hbm(w_down))


def small_copies(sources, out_shapes):
    arrays = [a for out in sources for a, _ in out]

    def body(*refs):
        given, outs, sem = list(refs[: len(arrays)]), refs[len(arrays) : -1], refs[-1]
        copies = []
        for out, blocks, (rows, _) in zip(outs, sources, out_shapes):
            rows //= len(blocks)
            for i, (_, first) in enumerate(blocks):
                copies.append(
                    pltpu.make_async_copy(
                        given.pop(0).at[pl.ds(first, rows), :],
                        out.at[pl.ds(i * rows, rows), :],
                        sem.at[len(copies)],
                    )
                )
        for copy in copies:
            copy.start()
        for copy in copies:
            copy.wait()

    return pl.pallas_call(
        body,
        in_specs=[HBM] * len(arrays),
        out_specs=[HBM] * len(out_shapes),
        out_shape=[pltpu.HBM(shape, BF16) for shape in out_shapes],
        scratch_shapes=[pltpu.SemaphoreType.DMA((len(arrays),))],
        cost_estimate=cost(0, 4 * sum(r * f for r, f in out_shapes)),
        compiler_params=pltpu.CompilerParams(vmem_limit_bytes=MIB),
        name="small_copies",
    )(*arrays)


def forward(xs, dys, per, weights):
    features, hidden = weights.shape[0], weights.shape[1] // 3
    rows = per * len(xs)
    tile = tile_of(features, 2048)
    steps = features // tile
    arrays = []
    for a, _ in xs + dys:
        if not any(a is b for b in arrays):
            arrays.append(a)
    place = [([a is b for b in arrays].index(True), r) for a, r in xs + dys]
    count = len(arrays)

    def body(*refs):
        sources = refs[:count]
        weight, own, rounded, held, sem = refs[count:]
        copies = []
        for k in range(steps):
            cut = pl.ds(k * tile, tile)
            for i, (a, r) in enumerate(place):
                copy = pltpu.make_async_copy(
                    sources[a].at[pl.ds(r * per, per), cut],
                    held.at[pl.ds(i * per, per), cut],
                    sem.at[k, i],
                )
                copy.start()
                copies.append(copy)
        for k in range(steps):
            cut = pl.ds(k * tile, tile)
            for i in range(len(place)):
                copies[k * len(place) + i].wait()
            for j in range(3):
                out = pl.ds(j * hidden, hidden)
                source = pl.ds(rows if j == 2 else 0, rows)
                part = dot(held[source, cut], weight[cut, out])
                if k == 0:
                    own[:, out] = part
                else:
                    own[:, out] += part
        rounded[...] = own[...].astype(BF16)

    return pl.pallas_call(
        body,
        in_specs=[HBM] * count + [VMEM],
        out_specs=[VMEM] * 2,
        out_shape=[
            jax.ShapeDtypeStruct((rows, 3 * hidden), F32),
            jax.ShapeDtypeStruct((rows, 3 * hidden), BF16),
        ],
        scratch_shapes=[
            pltpu.VMEM((2 * rows, features), BF16),
            pltpu.SemaphoreType.DMA((steps, len(place))),
        ],
        cost_estimate=cost(6 * rows * hidden * features, 6 * hidden * features),
        compiler_params=pltpu.CompilerParams(vmem_limit_bytes=12 * MIB),
        name="forward",
    )(*arrays, in_vmem(weights))


def backward(pairs, weights):
    features, hidden = weights.shape[0], weights.shape[1] // 3
    sizes = [own.shape[0] for own, _ in pairs]
    rows = sum(sizes)
    half, tile = rows // 2, tile_of(features, 1024)
    steps = features // tile
    padded = -(-rows // 128) * 128
    starts = [sum(sizes[:i]) for i in range(len(sizes))]

    def body(*refs):
        sums, refs = refs[: 2 * len(pairs)], refs[2 * len(pairs) :]
        weight, gate_to, up_to, act_to, mine, theirs = refs[:6]
        gate_out, up_out, act_out, turned, held, held16, sem, out_sem = refs[6:]
        for i, size in enumerate(sizes):
            own, other, at = sums[2 * i], sums[2 * i + 1], pl.ds(starts[i], size)

            def total(j, own=own, other=other):
                cut = pl.ds(j * hidden, hidden)
                return own[:, cut] + other[:, cut].astype(F32)

            gate_value, up_value, grad_act = total(0), total(1), total(2)
            sigmoid_gate = jax.nn.sigmoid(gate_value)
            silu_gate = gate_value * sigmoid_gate
            act_out[at, :] = (silu_gate * up_value).astype(BF16)
            up_out[at, :] = (grad_act * silu_gate).astype(BF16)
            gate_out[at, :] = (
                grad_act * up_value * sigmoid_gate * (1.0 + gate_value * (1.0 - sigmoid_gate))
            ).astype(BF16)
        copies = [
            pltpu.make_async_copy(source, target, out_sem.at[j])
            for j, (source, target) in enumerate(
                ((gate_out, gate_to), (up_out, up_to), (act_out, act_to))
            )
        ]
        for copy in copies:
            copy.start()
        if padded > rows:
            turned[:, rows:] = jnp.zeros((2 * hidden, padded - rows), BF16)
        turned[:hidden, :rows] = gate_out[...].T
        turned[hidden:, :rows] = up_out[...].T
        for k in range(steps):
            cut = pl.ds(k * tile, tile)
            out = dot(weight[cut, pl.ds(0, 2 * hidden)], turned[...]).T
            for start, size in zip(starts, sizes):
                to, middle = pl.ds(start // 2, size // 2), start + size // 2
                held[to, cut] = out[start:middle]
                held16[to, cut] = out[middle : start + size].astype(BF16)
            for j, (source, target) in enumerate(((held, mine), (held16, theirs))):
                copy = pltpu.make_async_copy(source.at[:, cut], target.at[:, cut], sem.at[k, j])
                copy.start()
                copies.append(copy)
        for copy in copies:
            copy.wait()

    return pl.pallas_call(
        body,
        in_specs=[VMEM] * (2 * len(pairs) + 1),
        out_specs=[HBM] * 5,
        out_shape=[pltpu.HBM((rows, hidden), BF16)] * 3
        + [pltpu.HBM((half, features), F32), pltpu.HBM((half, features), BF16)],
        scratch_shapes=[pltpu.VMEM((rows, hidden), BF16)] * 3
        + [
            pltpu.VMEM((2 * hidden, padded), BF16),
            pltpu.VMEM((half, features), F32),
            pltpu.VMEM((half, features), BF16),
            pltpu.SemaphoreType.DMA((steps, 2)),
            pltpu.SemaphoreType.DMA((3,)),
        ],
        cost_estimate=cost(4 * rows * hidden * features, 4 * hidden * features),
        compiler_params=pltpu.CompilerParams(vmem_limit_bytes=12 * MIB),
        name="backward",
    )(*[a for pair in pairs for a in pair], in_vmem(weights))


def part_of(part, features):
    start, size = (n * features // 8 for n in part)
    tile = math.gcd(math.gcd(start, size), 1024)
    return tile, start // tile, size // tile


def piece_specs(pieces, per, tile, first):
    return [pl.BlockSpec((per, tile), lambda i, r=r: (r, first + i)) for _, r in pieces]


def weight_grads_in(xs, per, grad_gates, grad_ups, part, before):
    rows, features = per * len(xs), xs[0][0].shape[1]
    hidden = grad_gates[0].shape[1]
    tile, first, steps = part_of(part, features)
    n_x, n_g = len(xs), len(grad_gates)

    def body(*refs):
        x = jnp.concatenate([r[...] for r in refs[:n_x]], 0)
        gate = jnp.concatenate([r[...] for r in refs[n_x : n_x + n_g]], 0)
        up = jnp.concatenate([r[...] for r in refs[n_x + n_g : n_x + 2 * n_g]], 0)
        out_gate, out_up = refs[-2:]
        out_gate[...] = dot_tn(x, gate).astype(BF16)
        out_up[...] = dot_tn(x, up).astype(BF16)

    whole = [pl.BlockSpec(g.shape, lambda i: (0, 0)) for g in grad_gates + grad_ups]
    out = pl.BlockSpec((tile, hidden), lambda i: (first + i, 0))
    given = [a for a, _ in xs] + grad_gates + grad_ups
    return pl.pallas_call(
        body,
        grid=(steps,),
        in_specs=piece_specs(xs, per, tile, first) + whole + [HBM] * len(before),
        out_specs=[out, out],
        out_shape=[jax.ShapeDtypeStruct((features, hidden), BF16)] * 2,
        input_output_aliases={len(given) + j: j for j in range(len(before))},
        cost_estimate=cost(
            4 * rows * hidden * steps * tile,
            (4 * hidden + 2 * rows) * steps * tile,
        ),
        compiler_params=pltpu.CompilerParams(vmem_limit_bytes=40 * MIB),
        name="weight_grads_in",
    )(*[in_hbm(a) for a in given], *before)


def weight_grad_out(activations, dys, per, part, before):
    rows, features = per * len(dys), dys[0][0].shape[1]
    hidden = activations[0].shape[1]
    tile, first, steps = part_of(part, features)
    n_y, n_a = len(dys), len(activations)

    def body(*refs):
        out, turned = refs[-2:]

        @pl.when(pl.program_id(0) == 0)
        def _():
            turned[...] = jnp.concatenate([r[...] for r in refs[n_y : n_y + n_a]], 0).T

        dy = jnp.concatenate([r[...] for r in refs[:n_y]], 0)
        out[...] = dot(turned[...], dy).astype(BF16)

    given = [a for a, _ in dys] + activations
    return pl.pallas_call(
        body,
        grid=(steps,),
        in_specs=piece_specs(dys, per, tile, first)
        + [pl.BlockSpec(a.shape, lambda i: (0, 0)) for a in activations]
        + [HBM] * len(before),
        out_specs=[pl.BlockSpec((hidden, tile), lambda i: (0, first + i))],
        out_shape=[jax.ShapeDtypeStruct((hidden, features), BF16)],
        input_output_aliases={len(given) + j: j for j in range(len(before))},
        scratch_shapes=[pltpu.VMEM((hidden, rows), BF16)],
        cost_estimate=cost(
            2 * rows * hidden * steps * tile,
            (2 * hidden + 2 * rows) * steps * tile,
        ),
        compiler_params=pltpu.CompilerParams(vmem_limit_bytes=40 * MIB),
        name="weight_grad_out",
    )(*[in_hbm(a) for a in given], *before)


def add_up(outs, rows, width):
    columns = [column for out in outs for column in out]
    given = [block for column in columns for block in column]
    tile = tile_of(width, 4096)
    steps = width // tile

    def body(*refs):
        sources, targets = list(refs[: len(given)]), refs[len(given) : len(given) + len(outs)]
        held, sem = refs[-2:]
        step = pl.program_id(0)
        at, copies = 0, []
        for target, out in zip(targets, outs):
            for j, column in enumerate(out):
                total = sources.pop(0)[...].astype(F32)
                for _ in column[1:]:
                    total = total + sources.pop(0)[...].astype(F32)
                held[at] = total.astype(BF16)
                cut = pl.ds(pl.multiple_of(j * width + step * tile, tile), tile)
                copies.append(pltpu.make_async_copy(held.at[at], target.at[:, cut], sem.at[at]))
                copies[-1].start()
                at += 1
        for copy in copies:
            copy.wait()

    return pl.pallas_call(
        body,
        grid=(steps,),
        in_specs=[
            pl.BlockSpec((rows, tile), lambda i, r=r, c=c: (r, c * steps + i)) for _, r, c in given
        ],
        out_specs=[HBM] * len(outs),
        out_shape=[jax.ShapeDtypeStruct((rows, len(out) * width), BF16) for out in outs],
        scratch_shapes=[
            pltpu.VMEM((len(columns), rows, tile), BF16),
            pltpu.SemaphoreType.DMA((len(columns),)),
        ],
        cost_estimate=cost(0, 4 * rows * width * len(given)),
        compiler_params=pltpu.CompilerParams(vmem_limit_bytes=24 * MIB),
        name="add_up",
    )(*[a for a, _, _ in given])


def make_local(rows, cols):
    chips = rows // 2
    far = chips // 2
    order = list(range(0, chips, 2)) + list(range(1, chips, 2))[::-1]

    def shift(by):
        return [
            (2 * order[k] + core, 2 * order[(k + by) % chips] + core)
            for k in range(chips)
            for core in (0, 1)
        ]

    to_next, to_prev = shift(1), shift(-1)
    swap = [(i, i ^ 1) for i in range(rows)]

    def right(a):
        return lax.ppermute(a, "row", to_next)

    def left(a):
        return lax.ppermute(a, "row", to_prev)

    def sibling(a):
        return lax.ppermute(a, "row", swap)

    def others(rounded):
        got = [
            lax.ppermute(rounded, "col", [(i, (i + by) % cols) for i in range(cols)])
            for by in range(1, cols)
        ]
        if len(got) == 1:
            return got[0]
        return sum(g.astype(F32) for g in got)

    def local(tokens, cotangent, w_gate, w_up, w_down):
        per, features = tokens.shape
        at = {0: jnp.concatenate([tokens, cotangent], 0)}
        weights = load_weights(w_gate, w_up, w_down)
        groups = [[0]] + [[k, -k] for k in range(1, far)] + [[far]]
        xs, dys, grads, reduced = [], [], [], {}

        def go_forward(group):
            if group == [far]:
                x, dy = at[far]
                x, dy = [(x, 0), (sibling(x), 0)], [(dy, 0), (sibling(dy), 0)]
            else:
                blocks = [at[k] for k in group] + [sibling(at[k]) for k in group]
                x, dy = [(b, 0) for b in blocks], [(b, 1) for b in blocks]
            xs.extend(x)
            dys.extend(dy)
            own, rounded = forward(x, dy, per, weights)
            if group not in (groups[0], groups[far]):
                rounded = after(rounded, latest[2])
            return group, own, others(rounded)

        def go_backward(*waiting):
            *grad, mine, theirs = backward([w[1:] for w in waiting], weights)
            grads.append(grad)
            theirs = sibling(theirs)
            for i, k in enumerate(k for w in waiting for k in w[0]):
                reduced[k] = [(in_hbm(mine) if far in waiting[-1][0] else mine, i), (theirs, i)]
            return mine

        at[-1], at[1] = right(at[0]), left(at[0])
        waiting = latest = go_forward(groups[0])
        done = [waiting[1]]
        for k in range(1, far):
            at[k], at[-k] = after((at[k], at[-k]), *done)
            if k + 1 < far:
                at[-k - 1], at[k + 1] = right(at[-k]), left(at[k])
            else:
                x, dy = small_copies([[(at[-k], 0)], [(at[k], per)]], [tokens.shape] * 2)
                at[far] = right(x), left(dy)
            latest = go_forward(groups[k])
            done = [latest[1]]
            if k + 1 < far:
                done.append(latest[2])
                done.append(go_backward((waiting[0], *after(waiting[1:], latest[1]))))
                waiting = latest
        at[far] = after(at[far], *done)
        last = go_forward(groups[far])
        done = go_backward((waiting[0], *after(waiting[1:], last[1])))
        go_backward((latest[0], *after(latest[1:], done)), last)

        gate_grads, up_grads, activations = ([g[i] for g in grads] for i in range(3))
        parts = [("out", 0, 2), ("in", 0, 4), ("in", 4, 4), ("out", 2, 5), ("out", 7, 1)]
        made = {"in": [], "out": []}

        def work():
            kind, *part = parts.pop(0)
            if kind == "in":
                made[kind] = weight_grads_in(xs, per, gate_grads, up_grads, part, made[kind])
            else:
                made[kind] = weight_grad_out(activations, dys, per, part, made[kind])

        def term(k, half):
            return [(a, i, half) for a, i in reduced[k]]

        came = {}
        work()
        for hop in range(far):
            outs, names = [], []
            for side, late in ((1, 0), (-1, 1)):
                out = []
                for half in (0, 1):
                    k = far - hop if half == late else far - 1 - hop
                    if k >= 1:
                        column = term(far if k == far else side * k, half)
                        names.append((side, half, len(out)))
                        out.append(column + came.get((side, half), []))
                outs.append(out)
            going = add_up(outs, per, features // 2)
            going, made = lax.optimization_barrier((going, made))
            going = {1: right(going[0]), -1: left(going[1])}
            for side, half, place in names:
                came[side, half] = [(going[side], 0, place)]
            if parts:
                work()
        while parts:
            work()
        last = [term(0, half) + came[1, half] + came[-1, half] for half in (0, 1)]
        (grad_tokens,) = add_up([last], per, features // 2)
        return (grad_tokens, *made["in"], *made["out"])

    return local


def solution(mesh):
    placed = (P("row", "col"), P("row", "col"), P("col", "row"), P("col", "row"), P("row", "col"))
    return jax.shard_map(
        make_local(mesh.shape["row"], mesh.shape["col"]),
        mesh=mesh,
        in_specs=placed,
        out_specs=(P("row", "col"), P("col", "row"), P("col", "row"), P("row", "col")),
        check_vma=False,
    )
```

```python
import math

import jax
import jax.numpy as jnp
from jax import lax
from jax.experimental import pallas as pl
from jax.experimental.pallas import tpu as pltpu
from jax.sharding import PartitionSpec as P

F32, BF16 = jnp.float32, jnp.bfloat16
MIB = 2**20
NT = (((1,), (1,)), ((), ()))
TN = (((0,), (0,)), ((), ()))
HBM = pl.BlockSpec(memory_space=pl.ANY)
VMEM = pl.BlockSpec(memory_space=pltpu.VMEM)


def dot(left, right):
    return jnp.dot(left, right, preferred_element_type=F32)


def dot_nt(left, right):
    return lax.dot_general(left, right, NT, preferred_element_type=F32)


def dot_tn(left, right):
    return lax.dot_general(left, right, TN, preferred_element_type=F32)


def tile_of(size, most):
    return most if size % most == 0 else size


def after(values, *earlier):
    return lax.optimization_barrier((values, earlier))[0]


def in_vmem(a):
    return pltpu.with_memory_space_constraint(a, pltpu.VMEM)


def in_hbm(a):
    return pltpu.with_memory_space_constraint(a, pltpu.HBM)


def cost(flops, nbytes):
    return pl.CostEstimate(flops=flops, bytes_accessed=nbytes, transcendentals=0)


def load_weights(w_gate, w_up, w_down):
    features, hidden = w_gate.shape
    tile = tile_of(features, 1024)
    steps = features // tile

    def body(gate, up, down, out, piece, sem, piece_sem):
        whole = [
            pltpu.make_async_copy(source, out.at[:, pl.ds(j * hidden, hidden)], sem.at[j])
            for j, source in enumerate((gate, up))
        ]
        pieces = [
            pltpu.make_async_copy(
                down.at[:, pl.ds(i * tile, tile)], piece.at[i % 2], piece_sem.at[i]
            )
            for i in range(steps)
        ]
        pieces[0].start()
        for copy in whole:
            copy.start()
        for i in range(steps):
            if i + 1 < steps:
                pieces[i + 1].start()
            pieces[i].wait()
            out[pl.ds(i * tile, tile), pl.ds(2 * hidden, hidden)] = piece[i % 2].T
        for copy in whole:
            copy.wait()

    return pl.pallas_call(
        body,
        in_specs=[HBM] * 3,
        out_specs=VMEM,
        out_shape=pltpu.VMEM((features, 3 * hidden), BF16),
        scratch_shapes=[
            pltpu.VMEM((2, hidden, tile), BF16),
            pltpu.SemaphoreType.DMA((2,)),
            pltpu.SemaphoreType.DMA((steps,)),
        ],
        cost_estimate=cost(0, 6 * features * hidden),
        compiler_params=pltpu.CompilerParams(vmem_limit_bytes=8 * MIB),
        name="load_weights",
    )(in_hbm(w_gate), in_hbm(w_up), in_hbm(w_down))


def small_copies(sources, out_shapes):
    arrays = [a for out in sources for a, _ in out]

    def body(*refs):
        given, outs, sem = list(refs[: len(arrays)]), refs[len(arrays) : -1], refs[-1]
        copies = []
        for out, blocks, (rows, _) in zip(outs, sources, out_shapes):
            rows //= len(blocks)
            for i, (_, first) in enumerate(blocks):
                copies.append(
                    pltpu.make_async_copy(
                        given.pop(0).at[pl.ds(first, rows), :],
                        out.at[pl.ds(i * rows, rows), :],
                        sem.at[len(copies)],
                    )
                )
        for copy in copies:
            copy.start()
        for copy in copies:
            copy.wait()

    return pl.pallas_call(
        body,
        in_specs=[HBM] * len(arrays),
        out_specs=[HBM] * len(out_shapes),
        out_shape=[pltpu.HBM(shape, BF16) for shape in out_shapes],
        scratch_shapes=[pltpu.SemaphoreType.DMA((len(arrays),))],
        cost_estimate=cost(0, 4 * sum(r * f for r, f in out_shapes)),
        compiler_params=pltpu.CompilerParams(vmem_limit_bytes=MIB),
        name="small_copies",
    )(*arrays)


def forward(xs, dys, per, weights):
    features, hidden = weights.shape[0], weights.shape[1] // 3
    rows = per * len(xs)
    tile = tile_of(features, 2048)
    steps = features // tile
    arrays = []
    for a, _ in xs + dys:
        if not any(a is b for b in arrays):
            arrays.append(a)
    place = [([a is b for b in arrays].index(True), r) for a, r in xs + dys]
    count = len(arrays)

    def body(*refs):
        sources = refs[:count]
        weight, own, rounded, held, sem = refs[count:]
        copies = []
        for k in range(steps):
            cut = pl.ds(k * tile, tile)
            for i, (a, r) in enumerate(place):
                copy = pltpu.make_async_copy(
                    sources[a].at[pl.ds(r * per, per), cut],
                    held.at[pl.ds(i * per, per), cut],
                    sem.at[k, i],
                )
                copy.start()
                copies.append(copy)
        for k in range(steps):
            cut = pl.ds(k * tile, tile)
            for i in range(len(place)):
                copies[k * len(place) + i].wait()
            for j in range(3):
                out = pl.ds(j * hidden, hidden)
                source = pl.ds(rows if j == 2 else 0, rows)
                part = dot(held[source, cut], weight[cut, out])
                if k == 0:
                    own[:, out] = part
                else:
                    own[:, out] += part
        rounded[...] = own[...].astype(BF16)

    return pl.pallas_call(
        body,
        in_specs=[HBM] * count + [VMEM],
        out_specs=[VMEM] * 2,
        out_shape=[
            jax.ShapeDtypeStruct((rows, 3 * hidden), F32),
            jax.ShapeDtypeStruct((rows, 3 * hidden), BF16),
        ],
        scratch_shapes=[
            pltpu.VMEM((2 * rows, features), BF16),
            pltpu.SemaphoreType.DMA((steps, len(place))),
        ],
        cost_estimate=cost(6 * rows * hidden * features, 6 * hidden * features),
        compiler_params=pltpu.CompilerParams(vmem_limit_bytes=12 * MIB),
        name="forward",
    )(*arrays, in_vmem(weights))


def backward(pairs, weights):
    features, hidden = weights.shape[0], weights.shape[1] // 3
    sizes = [own.shape[0] for own, _ in pairs]
    rows = sum(sizes)
    half, tile = rows // 2, tile_of(features, 1024)
    steps = features // tile
    padded = -(-rows // 128) * 128
    starts = [sum(sizes[:i]) for i in range(len(sizes))]

    def body(*refs):
        sums, refs = refs[: 2 * len(pairs)], refs[2 * len(pairs) :]
        weight, gate_to, up_to, act_to, mine, theirs = refs[:6]
        gate_out, up_out, act_out, turned, held, held16, sem, out_sem = refs[6:]
        for i, size in enumerate(sizes):
            own, other, at = sums[2 * i], sums[2 * i + 1], pl.ds(starts[i], size)

            def total(j, own=own, other=other):
                cut = pl.ds(j * hidden, hidden)
                return own[:, cut] + other[:, cut].astype(F32)

            gate_value, up_value, grad_act = total(0), total(1), total(2)
            sigmoid_gate = jax.nn.sigmoid(gate_value)
            silu_gate = gate_value * sigmoid_gate
            act_out[at, :] = (silu_gate * up_value).astype(BF16)
            up_out[at, :] = (grad_act * silu_gate).astype(BF16)
            gate_out[at, :] = (
                grad_act * up_value * sigmoid_gate * (1.0 + gate_value * (1.0 - sigmoid_gate))
            ).astype(BF16)
        copies = [
            pltpu.make_async_copy(source, target, out_sem.at[j])
            for j, (source, target) in enumerate(
                ((gate_out, gate_to), (up_out, up_to), (act_out, act_to))
            )
        ]
        for copy in copies:
            copy.start()
        if padded > rows:
            turned[:, rows:] = jnp.zeros((2 * hidden, padded - rows), BF16)
        turned[:hidden, :rows] = gate_out[...].T
        turned[hidden:, :rows] = up_out[...].T
        for k in range(steps):
            cut = pl.ds(k * tile, tile)
            out = dot(weight[cut, pl.ds(0, 2 * hidden)], turned[...]).T
            for start, size in zip(starts, sizes):
                to, middle = pl.ds(start // 2, size // 2), start + size // 2
                held[to, cut] = out[start:middle]
                held16[to, cut] = out[middle : start + size].astype(BF16)
            for j, (source, target) in enumerate(((held, mine), (held16, theirs))):
                copy = pltpu.make_async_copy(source.at[:, cut], target.at[:, cut], sem.at[k, j])
                copy.start()
                copies.append(copy)
        for copy in copies:
            copy.wait()

    return pl.pallas_call(
        body,
        in_specs=[VMEM] * (2 * len(pairs) + 1),
        out_specs=[HBM] * 5,
        out_shape=[pltpu.HBM((rows, hidden), BF16)] * 3
        + [pltpu.HBM((half, features), F32), pltpu.HBM((half, features), BF16)],
        scratch_shapes=[pltpu.VMEM((rows, hidden), BF16)] * 3
        + [
            pltpu.VMEM((2 * hidden, padded), BF16),
            pltpu.VMEM((half, features), F32),
            pltpu.VMEM((half, features), BF16),
            pltpu.SemaphoreType.DMA((steps, 2)),
            pltpu.SemaphoreType.DMA((3,)),
        ],
        cost_estimate=cost(4 * rows * hidden * features, 4 * hidden * features),
        compiler_params=pltpu.CompilerParams(vmem_limit_bytes=12 * MIB),
        name="backward",
    )(*[a for pair in pairs for a in pair], in_vmem(weights))


def part_of(part, features):
    start, size = (n * features // 8 for n in part)
    tile = math.gcd(math.gcd(start, size), 1024)
    return tile, start // tile, size // tile


def piece_specs(pieces, per, tile, first):
    return [pl.BlockSpec((per, tile), lambda i, r=r: (r, first + i)) for _, r in pieces]


def weight_grads_in(xs, per, grad_gates, grad_ups, part, before):
    rows, features = per * len(xs), xs[0][0].shape[1]
    hidden = grad_gates[0].shape[1]
    tile, first, steps = part_of(part, features)
    n_x, n_g = len(xs), len(grad_gates)

    def body(*refs):
        x = jnp.concatenate([r[...] for r in refs[:n_x]], 0)
        gate = jnp.concatenate([r[...] for r in refs[n_x : n_x + n_g]], 0)
        up = jnp.concatenate([r[...] for r in refs[n_x + n_g : n_x + 2 * n_g]], 0)
        out_gate, out_up = refs[-2:]
        out_gate[...] = dot_tn(x, gate).astype(BF16)
        out_up[...] = dot_tn(x, up).astype(BF16)

    whole = [pl.BlockSpec(g.shape, lambda i: (0, 0)) for g in grad_gates + grad_ups]
    out = pl.BlockSpec((tile, hidden), lambda i: (first + i, 0))
    given = [a for a, _ in xs] + grad_gates + grad_ups
    return pl.pallas_call(
        body,
        grid=(steps,),
        in_specs=piece_specs(xs, per, tile, first) + whole + [HBM] * len(before),
        out_specs=[out, out],
        out_shape=[jax.ShapeDtypeStruct((features, hidden), BF16)] * 2,
        input_output_aliases={len(given) + j: j for j in range(len(before))},
        cost_estimate=cost(
            4 * rows * hidden * steps * tile,
            (4 * hidden + 2 * rows) * steps * tile,
        ),
        compiler_params=pltpu.CompilerParams(vmem_limit_bytes=40 * MIB),
        name="weight_grads_in",
    )(*[in_hbm(a) for a in given], *before)


def weight_grad_out(activations, dys, per, part, before):
    rows, features = per * len(dys), dys[0][0].shape[1]
    hidden = activations[0].shape[1]
    tile, first, steps = part_of(part, features)
    n_y, n_a = len(dys), len(activations)

    def body(*refs):
        out, turned = refs[-2:]

        @pl.when(pl.program_id(0) == 0)
        def _():
            turned[...] = jnp.concatenate([r[...] for r in refs[n_y : n_y + n_a]], 0).T

        dy = jnp.concatenate([r[...] for r in refs[:n_y]], 0)
        out[...] = dot(turned[...], dy).astype(BF16)

    given = [a for a, _ in dys] + activations
    return pl.pallas_call(
        body,
        grid=(steps,),
        in_specs=piece_specs(dys, per, tile, first)
        + [pl.BlockSpec(a.shape, lambda i: (0, 0)) for a in activations]
        + [HBM] * len(before),
        out_specs=[pl.BlockSpec((hidden, tile), lambda i: (0, first + i))],
        out_shape=[jax.ShapeDtypeStruct((hidden, features), BF16)],
        input_output_aliases={len(given) + j: j for j in range(len(before))},
        scratch_shapes=[pltpu.VMEM((hidden, rows), BF16)],
        cost_estimate=cost(
            2 * rows * hidden * steps * tile,
            (2 * hidden + 2 * rows) * steps * tile,
        ),
        compiler_params=pltpu.CompilerParams(vmem_limit_bytes=40 * MIB),
        name="weight_grad_out",
    )(*[in_hbm(a) for a in given], *before)


def add_up(outs, rows, width):
    columns = [column for out in outs for column in out]
    given = [block for column in columns for block in column]
    tile = tile_of(width, 4096)
    steps = width // tile

    def body(*refs):
        sources, targets = list(refs[: len(given)]), refs[len(given) : len(given) + len(outs)]
        held, sem = refs[-2:]
        step = pl.program_id(0)
        at, copies = 0, []
        for target, out in zip(targets, outs):
            for j, column in enumerate(out):
                total = sources.pop(0)[...].astype(F32)
                for _ in column[1:]:
                    total = total + sources.pop(0)[...].astype(F32)
                held[at] = total.astype(BF16)
                cut = pl.ds(pl.multiple_of(j * width + step * tile, tile), tile)
                copies.append(pltpu.make_async_copy(held.at[at], target.at[:, cut], sem.at[at]))
                copies[-1].start()
                at += 1
        for copy in copies:
            copy.wait()

    return pl.pallas_call(
        body,
        grid=(steps,),
        in_specs=[
            pl.BlockSpec((rows, tile), lambda i, r=r, c=c: (r, c * steps + i)) for _, r, c in given
        ],
        out_specs=[HBM] * len(outs),
        out_shape=[jax.ShapeDtypeStruct((rows, len(out) * width), BF16) for out in outs],
        scratch_shapes=[
            pltpu.VMEM((len(columns), rows, tile), BF16),
            pltpu.SemaphoreType.DMA((len(columns),)),
        ],
        cost_estimate=cost(0, 4 * rows * width * len(given)),
        compiler_params=pltpu.CompilerParams(vmem_limit_bytes=24 * MIB),
        name="add_up",
    )(*[a for a, _, _ in given])


def make_local(rows, cols):
    chips = rows // 2
    far = chips // 2
    order = list(range(0, chips, 2)) + list(range(1, chips, 2))[::-1]

    def shift(by):
        return [
            (2 * order[k] + core, 2 * order[(k + by) % chips] + core)
            for k in range(chips)
            for core in (0, 1)
        ]

    to_next, to_prev = shift(1), shift(-1)
    swap = [(i, i ^ 1) for i in range(rows)]

    def right(a):
        return lax.ppermute(a, "row", to_next)

    def left(a):
        return lax.ppermute(a, "row", to_prev)

    def sibling(a):
        return lax.ppermute(a, "row", swap)

    def others(rounded):
        got = [
            lax.ppermute(rounded, "col", [(i, (i + by) % cols) for i in range(cols)])
            for by in range(1, cols)
        ]
        if len(got) == 1:
            return got[0]
        return sum(g.astype(F32) for g in got)

    def local(tokens, cotangent, w_gate, w_up, w_down):
        per, features = tokens.shape
        at = {0: jnp.concatenate([tokens, cotangent], 0)}
        weights = load_weights(w_gate, w_up, w_down)
        groups = [[0]] + [[k, -k] for k in range(1, far)] + [[far]]
        xs, dys, grads, reduced = [], [], [], {}

        def go_forward(group):
            if group == [far]:
                x, dy = at[far]
                x, dy = [(x, 0), (sibling(x), 0)], [(dy, 0), (sibling(dy), 0)]
            else:
                blocks = [at[k] for k in group] + [sibling(at[k]) for k in group]
                x, dy = [(b, 0) for b in blocks], [(b, 1) for b in blocks]
            xs.extend(x)
            dys.extend(dy)
            own, rounded = forward(x, dy, per, weights)
            if group not in (groups[0], groups[far]):
                rounded = after(rounded, latest[2])
            return group, own, others(rounded)

        def go_backward(*waiting):
            *grad, mine, theirs = backward([w[1:] for w in waiting], weights)
            grads.append(grad)
            theirs = sibling(theirs)
            for i, k in enumerate(k for w in waiting for k in w[0]):
                reduced[k] = [(in_hbm(mine) if far in waiting[-1][0] else mine, i), (theirs, i)]
            return mine

        at[-1], at[1] = right(at[0]), left(at[0])
        waiting = latest = go_forward(groups[0])
        done = [waiting[1]]
        for k in range(1, far):
            at[k], at[-k] = after((at[k], at[-k]), *done)
            if k + 1 < far:
                at[-k - 1], at[k + 1] = right(at[-k]), left(at[k])
            else:
                x, dy = small_copies([[(at[-k], 0)], [(at[k], per)]], [tokens.shape] * 2)
                at[far] = right(x), left(dy)
            latest = go_forward(groups[k])
            done = [latest[1]]
            if k + 1 < far:
                done.append(latest[2])
                done.append(go_backward((waiting[0], *after(waiting[1:], latest[1]))))
                waiting = latest
        at[far] = after(at[far], *done)
        last = go_forward(groups[far])
        done = go_backward((waiting[0], *after(waiting[1:], last[1])))
        go_backward((latest[0], *after(latest[1:], done)), last)

        gate_grads, up_grads, activations = ([g[i] for g in grads] for i in range(3))
        parts = [("out", 0, 2), ("in", 0, 4), ("in", 4, 4), ("out", 2, 4), ("out", 6, 2)]
        made = {"in": [], "out": []}

        def work():
            kind, *part = parts.pop(0)
            if kind == "in":
                made[kind] = weight_grads_in(xs, per, gate_grads, up_grads, part, made[kind])
            else:
                made[kind] = weight_grad_out(activations, dys, per, part, made[kind])

        def term(k, half):
            return [(a, i, half) for a, i in reduced[k]]

        came = {}
        work()
        for hop in range(far):
            outs, names = [], []
            for side, late in ((1, 0), (-1, 1)):
                out = []
                for half in (0, 1):
                    k = far - hop if half == late else far - 1 - hop
                    if k >= 1:
                        column = term(far if k == far else side * k, half)
                        names.append((side, half, len(out)))
                        out.append(column + came.get((side, half), []))
                outs.append(out)
            going = add_up(outs, per, features // 2)
            going, made = lax.optimization_barrier((going, made))
            going = {1: right(going[0]), -1: left(going[1])}
            for side, half, place in names:
                came[side, half] = [(going[side], 0, place)]
            if parts:
                work()
        while parts:
            work()
        last = [term(0, half) + came[1, half] + came[-1, half] for half in (0, 1)]
        (grad_tokens,) = add_up([last], per, features // 2)
        return (grad_tokens, *made["in"], *made["out"])

    return local


def solution(mesh):
    placed = (P("row", "col"), P("row", "col"), P("col", "row"), P("col", "row"), P("row", "col"))
    return jax.shard_map(
        make_local(mesh.shape["row"], mesh.shape["col"]),
        mesh=mesh,
        in_specs=placed,
        out_specs=(P("row", "col"), P("col", "row"), P("col", "row"), P("row", "col")),
        check_vma=False,
    )
```
